256 devices in a mesh: elem: 128 (over y, x, z), lev: 2 (over core).
Axes of the slice: x: 4, y: 4, z: 8, core: 2. Of those that a mesh axis runs over, the one named last changes fastest.
Arguments:
- tracers: bfloat16 [40, 72, 1024, 128], P(None, 'lev', 'elem'), may hold values from -6 to 6
- wind_x: bfloat16 [72, 1024, 128], P('lev', 'elem'), may hold values from -4 to 4
- wind_y: bfloat16 [72, 1024, 128], P('lev', 'elem'), may hold values from -4 to 4
- span_of: int32 [131072, 1], P('elem'), may hold values from 0 to 1023; in each aligned block of 1024 rows (0 to 1023, 1024 to 2047, ...) at most 2 rows name the same one
- inverses: bfloat16 [1024, 72, 72], P('elem'), may hold values from -2 to 2
Outputs:
- diffused: bfloat16 [40, 72, 1024, 128], P(None, 'lev', 'elem')
The draws below stay inside these ranges and needn't reach their ends.
Inputs may be any that keep to these rules, and one draw needn't show every extreme that they name: `span_of`: among the columns of one index of elem, at most 2 name the same span, a bound that some block reaches of them.
All inputs are finite; a program needn't handle non-finite values.
Results may differ from the reference program's by a relative error of at most 0.0049.
Values may be sent and summed in bfloat16 or wider, within the bound.
No kernel may reach another device: no remote copies, remote signals or barrier semaphores. Data moves between devices by JAX's collectives and lax.ppermute only.
A program may use at most 128 MiB of HBM per device.

```python
import math
import jax
import jax.numpy as jnp
import numpy as np
from jax import lax

Q = 40
LEV = 72
NP = 4
NSUB = 2
COLS_DEV = 1024
NX = 1024
NYN = 128
COLUMNS = 131072
SPANS = 1024
CAPC = 2
N_ELEM = 128


def draw_inverses(key, part):
    key = jax.random.fold_in(key, 7)
    key_main, key_side = jax.random.split(key)
    identity = jnp.eye(LEV, dtype=jnp.float32)
    diagonal = jax.random.uniform(key_main, (SPANS, LEV), jnp.float32, 0.5, 1.0)
    spread_part = jax.random.normal(key_side, (SPANS, LEV, LEV), jnp.float32) * (0.5 / math.sqrt(LEV))
    spread_part = jnp.clip(spread_part, -0.9, 0.9)
    matrices = spread_part * (1.0 - identity) + identity * diagonal[:, :, None]
    return matrices.astype(jnp.bfloat16)


def block_levels(rng, extent, cuts, low, largest):
    def one(position, blocks):
        heights = jax.random.uniform(jax.random.fold_in(jax.random.fold_in(rng, 6), position), (blocks,), jnp.float32, low / len(cuts), largest / len(cuts))
        return jnp.repeat(jnp.exp(heights), extent[position] // blocks).reshape((-1,) + (1,) * (len(extent) - position - 1))

    gain = one(*cuts[0])
    for cut in cuts[1:]:
        gain = gain * one(*cut)
    return gain


def shared_out(stream_key, own, number, rows, number_of, top, reach, slope):
    ranking = jax.random.permutation(stream_key, number_of)
    packed, common = shares(number_of, rows * top, reach, slope, True), shares(number_of, rows * top, reach, slope, False)
    places = jnp.arange(number_of)

    def named(tallies, turn):
        used = int((tallies > 0).sum())
        fixed = max(1, used // 4)
        moved = fixed + (places - fixed + turn * (used - fixed)) % max(1, number_of - fixed)
        return jnp.zeros((number_of,), jnp.int32).at[ranking[jnp.where(places < fixed, places, moved)]].set(jnp.asarray(tallies, jnp.int32))

    tallies = jnp.where(number % 4 == 0, named(packed, number // 4), named(common, number - number // 4 - 1))
    mixed = jax.random.permutation(jax.random.fold_in(own, 3), number_of)
    source_of, receiver = mixed[0:number_of // 2 * 2:2], mixed[1:number_of // 2 * 2:2]
    margin = jnp.minimum(tallies[source_of] - 1, reach - tallies[receiver]) // 2
    margin = jnp.where((source_of == ranking[0]) | (receiver == ranking[0]) | (tallies[receiver] == 0), 0, jnp.maximum(margin, 0))
    moved = jax.random.randint(jax.random.fold_in(own, 4), (number_of // 2,), 0, 1 << 20) % (margin + 1)
    tallies = tallies.at[source_of].add(-moved).at[receiver].add(moved)
    items = jnp.searchsorted(jnp.cumsum(tallies), jnp.arange(rows * top), side="right").astype(jnp.int32)
    listing = items.reshape(top, rows).T
    listing = listing[jax.random.permutation(jax.random.fold_in(own, 1), rows)]
    turn = jax.random.randint(jax.random.fold_in(own, 2), (rows, 1), 0, top)
    return jnp.take_along_axis(listing, (jnp.arange(top)[None, :] + turn) % top, axis=1)


def shares(amount, total, reach, skew, full):
    weights = [(1 << 20) // math.isqrt(standing ** skew) + 1 for standing in range(1, amount + 1)]
    largest = reach if full else min(reach, max(-(-total // amount), total * weights[0] // sum(weights)))
    least = 1 if total - largest >= amount - 1 else 0
    counts, surplus = [largest] + [least] * (amount - 1), total - largest - least * (amount - 1)
    while surplus > 0:
        movable = [i for i in range(1, amount) if counts[i] < largest] or [i for i in range(1, amount) if counts[i] < reach]
        whole, left = sum([weights[i] for i in movable]), surplus
        for i in movable:
            addition = min(reach - counts[i], max(1, left * weights[i] // whole), surplus)
            counts[i] = counts[i] + addition
            surplus = surplus - addition
    return np.array(counts)


def noise(stream_key, shape, spread, reach, cuts=(), kind=jnp.bfloat16):
    entries = jax.random.normal(stream_key, shape, jnp.float32) * spread
    if len(cuts) > 0:
        entries = block_levels(stream_key, shape, cuts, -0.22, 0.18) * entries
    return jnp.clip(entries, min=-reach, max=reach).astype(kind)


def setup_inputs(seed: int = 0) -> dict:
    key_of = jax.random.split(jax.random.key(seed), 6)
    tracers = noise(key_of[0], (Q, LEV, NX, NYN), 1.0, 6.0, ((1, 2), (2, 128)))
    wind_x = noise(key_of[1], (LEV, NX, NYN), 1.0, 4.0, ((0, 2), (1, 128)))
    wind_y = noise(key_of[2], (LEV, NX, NYN), 1.0, 4.0, ((0, 2), (1, 128)))
    span_of_keys = jax.random.split(jax.random.fold_in(key_of[3], 1), COLUMNS // COLS_DEV)
    span_of_turns = jax.random.permutation(jax.random.fold_in(key_of[3], 3), COLUMNS // COLS_DEV)
    span_of = jax.vmap(lambda own, number: shared_out(jax.random.fold_in(key_of[3], 2), own, number, COLS_DEV, SPANS, 1, CAPC, 2))(span_of_keys, span_of_turns).reshape((COLUMNS, 1))
    inverses = draw_inverses(jax.random.fold_in(key_of[5], 71), 0)
    return {"tracers": tracers, "wind_x": wind_x, "wind_y": wind_y, "span_of": span_of, "inverses": inverses}


time_step = 0.08

def derivative_table():
    gll_nodes = np.array([-1.0, -1.0 / np.sqrt(5.0), 1.0 / np.sqrt(5.0), 1.0])
    n = gll_nodes.shape[0]
    derivative = np.zeros((n, n))
    for i in range(n):
        for k in range(n):
            if i == k:
                derivative[i, k] = sum((1.0 / (gll_nodes[i] - gll_nodes[m]) for m in range(n) if m != i))
            else:
                numerator = np.prod([gll_nodes[i] - gll_nodes[m] for m in range(n) if m != k and m != i])
                denominator = np.prod([gll_nodes[k] - gll_nodes[m] for m in range(n) if m != k])
                derivative[i, k] = numerator / denominator
    return derivative.astype(np.float32)

def advance(field_state, derivative, winds_x, winds_y):
    groups, levels, width_x, width_y = field_state.shape
    full_shape = field_state.shape
    blocked = field_state.reshape(groups, levels, width_x // NP, NP, width_y)
    grad_x = jnp.einsum('ik,qlekn->qlein', derivative, blocked, precision=lax.Precision.HIGHEST).reshape(full_shape)
    blocked = field_state.reshape(groups, levels, width_x, width_y // NP, NP)
    grad_y = jnp.einsum('jk,qlxgk->qlxgj', derivative, blocked, precision=lax.Precision.HIGHEST).reshape(full_shape)
    advected = field_state - time_step * (winds_x * grad_x + winds_y * grad_y)
    blocked = advected.reshape(groups, levels, width_x // NP, NP, width_y)
    leading_nodes = blocked[:, :, :, 0]
    trailing_nodes = blocked[:, :, :, NP - 1]
    averaged = 0.5 * (trailing_nodes + jnp.roll(leading_nodes, -1, axis=2))
    blocked = blocked.at[:, :, :, NP - 1].set(averaged).at[:, :, :, 0].set(jnp.roll(averaged, 1, axis=2))
    blocked = blocked.reshape(groups, levels, width_x, width_y // NP, NP)
    leading_nodes = blocked[:, :, :, :, 0]
    trailing_nodes = blocked[:, :, :, :, NP - 1]
    averaged = 0.5 * (trailing_nodes + jnp.roll(leading_nodes, -1, axis=3))
    blocked = blocked.at[:, :, :, :, NP - 1].set(averaged).at[:, :, :, :, 0].set(jnp.roll(averaged, 1, axis=3))
    return blocked.reshape(full_shape)

def reference(tracers, wind_x, wind_y, span_of, inverses):
    derivative = jnp.asarray(derivative_table())
    winds_x = wind_x.astype(jnp.float32)[None]
    winds_y = wind_y.astype(jnp.float32)[None]
    field_state = tracers.astype(jnp.float32)
    for substep in range(NSUB):
        field_state = advance(field_state, derivative, winds_x, winds_y)
    dynamics = field_state.astype(jnp.bfloat16).reshape(Q, LEV, COLUMNS)
    span_ids = span_of[:, 0].astype(jnp.int32)

    def solve(block_index):
        offset = (block_index * COLS_DEV).astype(jnp.int32)
        portion = lax.dynamic_slice_in_dim(dynamics, offset, COLS_DEV, 2).astype(jnp.float32)
        picked_ids = lax.dynamic_slice_in_dim(span_ids, offset, COLS_DEV, 0)
        matrices = jnp.take(inverses, picked_ids, axis=0).astype(jnp.float32)
        return jnp.einsum('cab,qbc->qac', matrices, portion).astype(jnp.bfloat16)
    solved = lax.map(solve, jnp.arange(N_ELEM, dtype=jnp.int32))
    return jnp.transpose(solved, (1, 2, 0, 3)).reshape(Q, LEV, NX, NYN)
```

```python
import jax
import jax.numpy as jnp
import numpy as np
from jax import lax
from jax.experimental import pallas as pl
from jax.experimental.pallas import tpu as pltpu
from jax.sharding import PartitionSpec as P

NP = 4
TIME_STEP = 0.08
NY_CHIPS, NX_CHIPS, NZ_CHIPS = 4, 4, 8
CHUNKS = 2
F32, BF16 = jnp.float32, jnp.bfloat16


def derivative_table():
    nodes = np.array([-1.0, -1.0 / np.sqrt(5.0), 1.0 / np.sqrt(5.0), 1.0])
    table = np.zeros((NP, NP))
    for i in range(NP):
        for k in range(NP):
            if i == k:
                table[i, k] = sum(1.0 / (nodes[i] - nodes[m]) for m in range(NP) if m != i)
            else:
                top = np.prod([nodes[i] - nodes[m] for m in range(NP) if m != k and m != i])
                table[i, k] = top / np.prod([nodes[k] - nodes[m] for m in range(NP) if m != k])
    return table


D = derivative_table()
D = [[float(D[i, k]) for k in range(NP)] for i in range(NP)]


def table_y(width):
    full = np.kron(np.eye(width // NP), np.array(D)).T.astype(np.float32)
    hi = full.astype(jnp.bfloat16)
    lo = (full - hi.astype(np.float32)).astype(jnp.bfloat16)
    first = np.concatenate([hi, lo], axis=0)
    zero = np.zeros_like(lo)
    second = np.concatenate(
        [np.concatenate([hi, lo], axis=1), np.concatenate([hi, zero], axis=1)], axis=0
    )
    return jnp.asarray(first), jnp.asarray(second)


def grad_x(s0, s1, s2, s3):
    m, n = s3 - s0, s2 - s1
    e = (s0 + s3) - (s1 + s2)
    a = 0.5 * (D[3][3] + D[0][3])
    b = 0.5 * (D[0][1] + D[3][1])
    u = a * m - b * n
    v = (0.5 * (D[1][3] + D[2][3])) * m + (0.5 * (D[1][2] + D[2][2])) * n
    w = (0.5 * (D[3][3] - D[0][3])) * e
    z = (0.5 * (D[2][3] - D[1][3])) * e
    return [u - w, v - z, v + z, u + w]


def mean_y(value, last, inner):
    width = value.shape[1]
    ahead = pltpu.roll(value, width - 1, axis=1)
    behind = pltpu.roll(value, 1, axis=1)
    return jnp.where(inner, value, 0.5 * (value + jnp.where(last, ahead, behind)))


def node_masks(shape):
    node = lax.broadcasted_iota(jnp.int32, shape, 1) % NP
    return node == NP - 1, (node == 1) | (node == 2)


def first_kernel(levels, t_ref, wx_ref, wy_ref, d_ref, st_ref, dn_ref, up_ref, scr):
    groups, width_x, width_y = t_ref.shape[0], t_ref.shape[2], t_ref.shape[3]
    last, inner = node_masks((groups, width_y))

    @pl.loop(0, levels)
    def _(l):
        scr[...] = t_ref[:, l].astype(F32).reshape(groups * width_x, width_y)
        s = [scr[pl.ds(x, groups, stride=width_x), :] for x in range(width_x)]
        wx = wx_ref[l].astype(F32) * TIME_STEP
        wy = wy_ref[l].astype(F32) * TIME_STEP
        flat = jnp.concatenate(s, axis=0).astype(BF16)
        gy = jnp.dot(
            jnp.concatenate([flat, flat], axis=1), d_ref[...], preferred_element_type=F32
        )
        gx = grad_x(*s[:4]) + grad_x(*s[4:])
        adv = [
            s[x]
            - (wx[x : x + 1] * gx[x] + wy[x : x + 1] * gy[x * groups : (x + 1) * groups])
            for x in range(width_x)
        ]
        middle = mean_y(0.5 * (adv[3] + adv[4]), last, inner)
        st = [adv[0], None, None, middle, middle, None, None, adv[7]]
        for x in (1, 2, 5, 6):
            st[x] = mean_y(adv[x], last, inner)
        for x in range(width_x):
            st_ref[l, x] = st[x]
        part = D[0][1] * st[1] + D[0][2] * st[2] + D[0][3] * st[3]
        dn_ref[l, 0] = adv[0].astype(BF16)
        dn_ref[l, 1] = (-wx[0:1] * part).astype(BF16)
        part = D[3][0] * st[4] + D[3][1] * st[5] + D[3][2] * st[6]
        up_ref[l, 0] = adv[7].astype(BF16)
        up_ref[l, 1] = (-wx[7:8] * part).astype(BF16)


def second_kernel(
    levels, st_ref, left_ref, right_ref, wx_ref, wy_ref, wl_ref, wr_ref, d_ref, out_ref
):
    width_x, groups, width_y = st_ref.shape[1:]
    last, inner = node_masks((groups, width_y))

    @pl.loop(0, levels)
    def _(l):
        s = [None] + [st_ref[l, x] for x in range(1, 7)] + [None]
        s[0] = mean_y(0.5 * (st_ref[l, 0] + left_ref[l, 0].astype(F32)), last, inner)
        s[7] = mean_y(0.5 * (st_ref[l, 7] + right_ref[l, 0].astype(F32)), last, inner)
        wx = wx_ref[l].astype(F32) * TIME_STEP
        wy = wy_ref[l].astype(F32) * TIME_STEP
        wl = wl_ref[l].astype(F32) * TIME_STEP
        wr = wr_ref[l].astype(F32) * TIME_STEP
        flat = jnp.concatenate(s, axis=0)
        hi = flat.astype(BF16)
        lo = (flat - hi.astype(F32)).astype(BF16)
        both = jnp.dot(
            jnp.concatenate([hi, lo], axis=1), d_ref[...], preferred_element_type=F32
        )
        gy = both[:, :width_y] + both[:, width_y:]
        gys = [gy[x * groups : (x + 1) * groups] for x in range(width_x)]
        gx = grad_x(*s[:4]) + grad_x(*s[4:])
        adv = [
            s[x] - (wx[x : x + 1] * gx[x] + wy[x : x + 1] * gys[x]) for x in range(width_x)
        ]
        before = (
            s[0]
            - ((wl[0:1] * D[3][3]) * s[0] + wl[1:2] * gys[0])
            + left_ref[l, 1].astype(F32)
        )
        after = (
            s[7]
            - ((wr[0:1] * D[0][0]) * s[7] + wr[1:2] * gys[7])
            + right_ref[l, 1].astype(F32)
        )
        middle = 0.5 * (adv[3] + adv[4])
        adv[0] = 0.5 * (before + adv[0])
        adv[7] = 0.5 * (adv[7] + after)
        adv[3] = middle
        for x in range(width_x):
            if x != 4:
                done = mean_y(adv[x], last, inner).astype(BF16)
                out_ref[l, x] = done
                if x == 3:
                    out_ref[l, 4] = done


def first_part(tracers, wind_x, wind_y, table, start, count):
    groups, _, width_x, width_y = tracers.shape
    step = 3
    skip = start // step
    spec_w = pl.BlockSpec((step, width_x, width_y), lambda i: (i + skip, 0, 0))
    spec_m = pl.BlockSpec((step, 2, groups, width_y), lambda i: (i, 0, 0, 0))
    return pl.pallas_call(
        lambda *refs: first_kernel(step, *refs),
        grid=(count // step,),
        in_specs=[
            pl.BlockSpec((groups, step, width_x, width_y), lambda i: (0, i + skip, 0, 0)),
            spec_w,
            spec_w,
            pl.BlockSpec(table.shape, lambda i: (0, 0)),
        ],
        out_specs=[
            pl.BlockSpec((step, width_x, groups, width_y), lambda i: (i, 0, 0, 0)),
            spec_m,
            spec_m,
        ],
        out_shape=[
            jax.ShapeDtypeStruct((count, width_x, groups, width_y), F32),
            jax.ShapeDtypeStruct((count, 2, groups, width_y), BF16),
            jax.ShapeDtypeStruct((count, 2, groups, width_y), BF16),
        ],
        scratch_shapes=[pltpu.VMEM((groups * width_x, width_y), F32)],
        compiler_params=pltpu.CompilerParams(vmem_limit_bytes=24 << 20),
        cost_estimate=pl.CostEstimate(
            flops=40 * count * width_x * groups * width_y,
            bytes_accessed=8 * count * width_x * groups * width_y,
            transcendentals=0,
        ),
        name="transport_first",
    )(tracers, wind_x, wind_y, table)


def second_part(state, left, right, wind_x, wind_y, wind_l, wind_r, table, start):
    count, width_x, groups, width_y = state.shape
    step = 3
    skip = start // step
    spec_s = pl.BlockSpec((step, width_x, groups, width_y), lambda i: (i, 0, 0, 0))
    spec_m = pl.BlockSpec((step, 2, groups, width_y), lambda i: (i, 0, 0, 0))
    spec_w = pl.BlockSpec((step, width_x, width_y), lambda i: (i + skip, 0, 0))
    spec_n = pl.BlockSpec((step, 2, width_y), lambda i: (i + skip, 0, 0))
    return pl.pallas_call(
        lambda *refs: second_kernel(step, *refs),
        grid=(count // step,),
        in_specs=[
            spec_s, spec_m, spec_m, spec_w, spec_w, spec_n, spec_n,
            pl.BlockSpec(table.shape, lambda i: (0, 0)),
        ],
        out_specs=spec_s,
        out_shape=jax.ShapeDtypeStruct(state.shape, BF16),
        compiler_params=pltpu.CompilerParams(vmem_limit_bytes=24 << 20),
        cost_estimate=pl.CostEstimate(
            flops=40 * count * width_x * groups * width_y,
            bytes_accessed=8 * count * width_x * groups * width_y,
            transcendentals=0,
        ),
        name="transport_second",
    )(state, left, right, wind_x, wind_y, wind_l, wind_r, table)


A_STEP = 6


def solve_kernel(n_fields, half_rows, pos_ref, *refs):
    fields = refs[:n_fields]
    pieces = refs[n_fields : n_fields + 10]
    out_ref = refs[n_fields + 10]
    value, choice, chosen, result = refs[n_fields + 11 :]
    width_x, groups, width_y = value.shape[1:]
    levels = value.shape[0]
    step = pl.program_id(0)
    half = pl.num_programs(0) // 2

    @pl.when(step == 0)
    def _():
        base = 0
        for field in fields:
            count = field.shape[0]

            @pl.loop(0, count)
            def _(l, base=base, field=field):
                for x in range(width_x):
                    value[base + l, x] = field[l, x].astype(F32)

            base += count
        spans = choice.shape[0]
        for x in range(width_x):
            for k in range(spans // 128):
                row = lax.broadcasted_iota(jnp.int32, (128, width_y), 0) + k * 128
                hit = row == pos_ref[x : x + 1, :]
                choice[k * 128 : (k + 1) * 128, x * width_y : (x + 1) * width_y] = (
                    jnp.where(hit, 1.0, 0.0).astype(BF16)
                )

    early = step < half
    blocks = []
    for group in range(2):
        a, b, lo, hi, c = pieces[group * 5 : group * 5 + 5]
        blocks += [a[...], b[...], jnp.where(early, lo[...], hi[...]), c[...]]
    matrices = jnp.concatenate(blocks, axis=1)
    for x in range(0, width_x, 2):
        cols = slice(x * width_y, (x + 2) * width_y)
        chosen[:, cols] = jnp.dot(matrices, choice[:, cols], preferred_element_type=F32)

    @pl.loop(0, width_x)
    def _(x):
        lanes = pl.ds(pl.multiple_of(x * width_y, width_y), width_y)
        for first in range(0, A_STEP, 3):
            total = [jnp.zeros((groups, width_y), F32)] * 3
            for b in range(levels):
                levels_b = value[b, x]
                for i in range(3):
                    row = (first + i) * levels + b
                    total[i] = total[i] + chosen[row : row + 1, lanes] * levels_b
            for i in range(3):
                result[first + i, pl.ds(x, groups, stride=width_x), :] = total[i]

    for a in range(A_STEP):
        out_ref[:, a] = result[a].reshape(groups, width_x, width_y).astype(BF16)


def solve(fields, pieces, position, groups, levels_out, width_x, width_y):
    levels = sum(f.shape[0] for f in fields)
    rows = A_STEP * levels
    steps = levels_out // A_STEP
    half = steps // 2
    full = pl.BlockSpec((rows, 128), lambda i: (i, 0))
    low = pl.BlockSpec((rows, 128), lambda i: (jnp.minimum(i, half - 1), 0))
    high = pl.BlockSpec((rows, 128), lambda i: (jnp.maximum(i - half, 0), 0))
    spans = 1024
    return pl.pallas_call(
        lambda *refs: solve_kernel(len(fields), rows * half, *refs),
        grid=(steps,),
        in_specs=[pl.BlockSpec(position.shape, lambda i: (0, 0))]
        + [pl.BlockSpec(f.shape, lambda i: (0, 0, 0, 0)) for f in fields]
        + [full, full, low, high, full] * 2,
        out_specs=pl.BlockSpec((groups, A_STEP, width_x, width_y), lambda i: (0, i, 0, 0)),
        out_shape=jax.ShapeDtypeStruct((groups, levels_out, width_x, width_y), BF16),
        scratch_shapes=[
            pltpu.VMEM((levels, width_x, groups, width_y), F32),
            pltpu.VMEM((spans, width_x * width_y), BF16),
            pltpu.VMEM((rows, width_x * width_y), F32),
            pltpu.VMEM((A_STEP, groups * width_x, width_y), F32),
        ],
        compiler_params=pltpu.CompilerParams(vmem_limit_bytes=48 << 20),
        cost_estimate=pl.CostEstimate(
            flops=2 * levels_out * levels * groups * width_x * width_y,
            bytes_accessed=12 << 20,
            transcendentals=0,
        ),
        name="solve_columns",
    )(position, *fields, *pieces)


def elem_index(y, x, z):
    return (y % NY_CHIPS * NX_CHIPS + x % NX_CHIPS) * NZ_CHIPS + z % NZ_CHIPS


def fetch(value, dy=0, dx=0, dz=0):
    pairs = [
        (elem_index(y + dy, x + dx, z + dz), elem_index(y, x, z))
        for y in range(NY_CHIPS)
        for x in range(NX_CHIPS)
        for z in range(NZ_CHIPS)
    ]
    return lax.ppermute(value, "elem", pairs)


def ring_of_four(value, axis, cut):
    ahead = fetch(value, **{axis: 1})
    behind = fetch(value, **{axis: -1})
    first = fetch(ahead[:cut], **{axis: 1})
    second = fetch(behind[cut:], **{axis: -1})
    return [value, ahead, first, second, behind]


def gather_matrices(rows):
    entries = rows.shape[1]
    cut = entries // 2
    near = [rows] + [fetch(rows, dz=d) for d in range(1, NZ_CHIPS)]
    pieces = []
    for group, (one, two) in enumerate((("dx", "dy"), ("dy", "dx"))):
        part = jnp.concatenate(near[group * 4 : group * 4 + 4], axis=0)
        value, ahead, first, second, behind = ring_of_four(part, one, part.shape[0] // 2)
        part = jnp.concatenate([value, ahead, first, second, behind], axis=0)
        pieces += ring_of_four(part.T, two, cut)
    return pieces


def span_position(span_ids, per_dev):
    here = lax.axis_index("elem")
    owner, local = span_ids // per_dev, span_ids % per_dev
    dz = (owner % NZ_CHIPS - here % NZ_CHIPS) % NZ_CHIPS
    dx = (owner // NZ_CHIPS % NX_CHIPS - here // NZ_CHIPS % NX_CHIPS) % NX_CHIPS
    dy = (owner // (NZ_CHIPS * NX_CHIPS) - here // (NZ_CHIPS * NX_CHIPS)) % NY_CHIPS
    inside = (dz % 4) * per_dev + local
    return jnp.where(
        dz < 4, dy * 128 + dx * 32 + inside, 512 + dx * 128 + dy * 32 + inside
    ).astype(jnp.int32)


def body(tracers, wind_x, wind_y, span_of, inverses):
    groups, half_levels, width_x, width_y = tracers.shape
    per_dev = inverses.shape[0]
    first_table, second_table = table_y(width_y)
    size = lax.axis_size("elem")
    up = [(i, (i + 1) % size) for i in range(size)]
    down = [(j, i) for i, j in up]
    lev = lax.axis_index("lev")

    mine = lax.dynamic_slice_in_dim(inverses, lev * half_levels, half_levels, 1)
    own = lax.dynamic_slice_in_dim(mine, lev * half_levels, half_levels, 2)
    other = lax.dynamic_slice_in_dim(mine, (1 - lev) * half_levels, half_levels, 2)
    rows = jnp.concatenate([own, other], axis=2).reshape(per_dev, -1)
    pieces = gather_matrices(rows)
    position = span_position(span_of[:, 0], per_dev).reshape(width_x, width_y)

    wind_l = lax.ppermute(jnp.stack([wind_x[:, -1], wind_y[:, -1]], 1), "elem", up)
    wind_r = lax.ppermute(jnp.stack([wind_x[:, 0], wind_y[:, 0]], 1), "elem", down)

    count = half_levels // CHUNKS
    firsts = [
        first_part(tracers, wind_x, wind_y, first_table, i * count, count)
        for i in range(CHUNKS)
    ]
    own_fields, other_fields = [], []
    for i, (state, to_left, to_right) in enumerate(firsts):
        left = lax.ppermute(to_right, "elem", up)
        right = lax.ppermute(to_left, "elem", down)
        field = second_part(
            state, left, right, wind_x, wind_y, wind_l, wind_r, second_table, i * count
        )
        own_fields.append(field)
        other_fields.append(lax.ppermute(field, "lev", [(0, 1), (1, 0)]))
    return solve(
        own_fields + other_fields, pieces, position, groups, half_levels, width_x, width_y
    )


def solution(mesh):
    return jax.shard_map(
        body,
        mesh=mesh,
        in_specs=(
            P(None, "lev", "elem", None),
            P("lev", "elem", None),
            P("lev", "elem", None),
            P("elem", None),
            P("elem", None, None),
        ),
        out_specs=P(None, "lev", "elem", None),
        check_vma=False,
    )
```

```python
import functools

import jax
import jax.numpy as jnp
import numpy as np
from jax import lax
from jax.experimental import pallas as pl
from jax.experimental.pallas import tpu as pltpu
from jax.sharding import PartitionSpec as P

NP = 4
TIME_STEP = 0.08
NY_CHIPS, NX_CHIPS, NZ_CHIPS = 4, 4, 8
ELEM = ("y", "x", "z")
CHUNKS = 2
LANES = 128
TRIPLES = ((0, 1, 2), (3, 4, 5), (6, 7))
HEIGHT = 48
F32, BF16 = jnp.float32, jnp.bfloat16


def derivative_table():
    nodes = np.array([-1.0, -1.0 / np.sqrt(5.0), 1.0 / np.sqrt(5.0), 1.0])
    table = np.zeros((NP, NP))
    for i in range(NP):
        for k in range(NP):
            if i == k:
                table[i, k] = sum(1.0 / (nodes[i] - nodes[m]) for m in range(NP) if m != i)
            else:
                top = np.prod([nodes[i] - nodes[m] for m in range(NP) if m != k and m != i])
                table[i, k] = top / np.prod([nodes[k] - nodes[m] for m in range(NP) if m != k])
    return table


D = derivative_table()
D = [[float(D[i, k]) for k in range(NP)] for i in range(NP)]


def table_y(width):
    full = np.kron(np.eye(width // NP), np.array(D)).T.astype(np.float32)
    hi = full.astype(jnp.bfloat16)
    lo = (full - hi.astype(np.float32)).astype(jnp.bfloat16)
    first = np.concatenate([hi, lo], axis=0)
    zero = np.zeros_like(lo)
    second = np.concatenate(
        [np.concatenate([hi, lo], axis=1), np.concatenate([hi, zero], axis=1)], axis=0
    )
    mean = np.eye(width)
    for y in range(width):
        if y % NP in (0, NP - 1):
            mean[y, y] = mean[y, (y + (1 if y % NP else -1)) % width] = 0.5
    mean = np.concatenate([mean, mean], axis=1).astype(jnp.bfloat16)
    return jnp.asarray(first), jnp.asarray(second), jnp.asarray(mean)


def grad_x(s0, s1, s2, s3):
    m, n = s3 - s0, s2 - s1
    e = (s0 + s3) - (s1 + s2)
    a = 0.5 * (D[3][3] + D[0][3])
    b = 0.5 * (D[0][1] + D[3][1])
    u = a * m - b * n
    v = (0.5 * (D[1][3] + D[2][3])) * m + (0.5 * (D[1][2] + D[2][2])) * n
    w = (0.5 * (D[3][3] - D[0][3])) * e
    z = (0.5 * (D[2][3] - D[1][3])) * e
    return [u - w, v - z, v + z, u + w]


def mean_y(value, last, inner):
    width = value.shape[1]
    ahead = pltpu.roll(value, width - 1, axis=1)
    behind = pltpu.roll(value, 1, axis=1)
    return jnp.where(inner, value, 0.5 * (value + jnp.where(last, ahead, behind)))


def node_masks(shape):
    node = lax.broadcasted_iota(jnp.int32, shape, 1) % NP
    return node == NP - 1, (node == 1) | (node == 2)


def first_kernel(levels, t_ref, wx_ref, wy_ref, d_ref, st_ref, dn_ref, up_ref, scr):
    groups, width_x, width_y = t_ref.shape[0], t_ref.shape[2], t_ref.shape[3]
    last, inner = node_masks((groups, width_y))

    @pl.loop(0, levels, unroll=3)
    def _(l):
        scr[...] = t_ref[:, l].astype(F32).reshape(groups * width_x, width_y)
        s = [scr[pl.ds(x, groups, stride=width_x), :] for x in range(width_x)]
        wx = wx_ref[l].astype(F32) * TIME_STEP
        wy = wy_ref[l].astype(F32) * TIME_STEP
        flat = jnp.concatenate(s, axis=0).astype(BF16)
        gy = jnp.dot(
            jnp.concatenate([flat, flat], axis=1), d_ref[...], preferred_element_type=F32
        )
        gx = grad_x(*s[:4]) + grad_x(*s[4:])
        adv = [
            s[x]
            - (wx[x : x + 1] * gx[x] + wy[x : x + 1] * gy[x * groups : (x + 1) * groups])
            for x in range(width_x)
        ]
        middle = mean_y(0.5 * (adv[3] + adv[4]), last, inner)
        st = [adv[0], None, None, middle, middle, None, None, adv[7]]
        for x in (1, 2, 5, 6):
            st[x] = mean_y(adv[x], last, inner)
        for x in range(width_x):
            st_ref[l, x] = st[x]
        part = D[0][1] * st[1] + D[0][2] * st[2] + D[0][3] * st[3]
        dn_ref[l, 0] = adv[0].astype(BF16)
        dn_ref[l, 1] = (-wx[0:1] * part).astype(BF16)
        part = D[3][0] * st[4] + D[3][1] * st[5] + D[3][2] * st[6]
        up_ref[l, 0] = adv[7].astype(BF16)
        up_ref[l, 1] = (-wx[7:8] * part).astype(BF16)


def second_kernel(
    levels, st_ref, left_ref, right_ref, wx_ref, wy_ref, wl_ref, wr_ref, d_ref, m_ref, out_ref
):
    width_x, groups, width_y = st_ref.shape[1:]
    last, inner = node_masks((groups, width_y))

    @pl.loop(0, levels, unroll=3)
    def _(l):
        s = [None] + [st_ref[l, x] for x in range(1, 7)] + [None]
        s[0] = mean_y(0.5 * (st_ref[l, 0] + left_ref[l, 0].astype(F32)), last, inner)
        s[7] = mean_y(0.5 * (st_ref[l, 7] + right_ref[l, 0].astype(F32)), last, inner)
        wx = wx_ref[l].astype(F32) * TIME_STEP
        wy = wy_ref[l].astype(F32) * TIME_STEP
        wl = wl_ref[l].astype(F32) * TIME_STEP
        wr = wr_ref[l].astype(F32) * TIME_STEP
        flat = jnp.concatenate(s, axis=0)
        hi = flat.astype(BF16)
        lo = (flat - hi.astype(F32)).astype(BF16)
        both = jnp.dot(
            jnp.concatenate([hi, lo], axis=1), d_ref[...], preferred_element_type=F32
        )
        gy = both[:, :width_y] + both[:, width_y:]
        gys = [gy[x * groups : (x + 1) * groups] for x in range(width_x)]
        gx = grad_x(*s[:4]) + grad_x(*s[4:])
        adv = [
            s[x] - (wx[x : x + 1] * gx[x] + wy[x : x + 1] * gys[x]) for x in range(width_x)
        ]
        before = (
            s[0]
            - ((wl[0:1] * D[3][3]) * s[0] + wl[1:2] * gys[0])
            + left_ref[l, 1].astype(F32)
        )
        after = (
            s[7]
            - ((wr[0:1] * D[0][0]) * s[7] + wr[1:2] * gys[7])
            + right_ref[l, 1].astype(F32)
        )
        middle = 0.5 * (adv[3] + adv[4])
        adv[0] = 0.5 * (before + adv[0])
        adv[7] = 0.5 * (adv[7] + after)
        adv[3] = adv[4] = middle
        for g, triple in enumerate(TRIPLES):
            rest = jnp.zeros((LANES - len(triple) * groups, width_y), F32)
            flat = jnp.concatenate([adv[x] for x in triple] + [rest], axis=0)
            hi = flat.astype(BF16)
            lo = (flat - hi.astype(F32)).astype(BF16)
            out_ref[l, g] = lax.dot_general(
                m_ref[...],
                jnp.concatenate([hi, lo], axis=1),
                (((1,), (1,)), ((), ())),
                preferred_element_type=F32,
            ).astype(BF16)


def first_part(tracers, wind_x, wind_y, table, start, count):
    groups, _, width_x, width_y = tracers.shape
    step = 3
    skip = start // step
    spec_w = pl.BlockSpec((step, width_x, width_y), lambda i: (i + skip, 0, 0))
    spec_m = pl.BlockSpec((step, 2, groups, width_y), lambda i: (i, 0, 0, 0))
    return pl.pallas_call(
        lambda *refs: first_kernel(step, *refs),
        grid=(count // step,),
        in_specs=[
            pl.BlockSpec((groups, step, width_x, width_y), lambda i: (0, i + skip, 0, 0)),
            spec_w,
            spec_w,
            pl.BlockSpec(table.shape, lambda i: (0, 0)),
        ],
        out_specs=[
            pl.BlockSpec((step, width_x, groups, width_y), lambda i: (i, 0, 0, 0)),
            spec_m,
            spec_m,
        ],
        out_shape=[
            jax.ShapeDtypeStruct((count, width_x, groups, width_y), F32),
            jax.ShapeDtypeStruct((count, 2, groups, width_y), BF16),
            jax.ShapeDtypeStruct((count, 2, groups, width_y), BF16),
        ],
        scratch_shapes=[pltpu.VMEM((groups * width_x, width_y), F32)],
        compiler_params=pltpu.CompilerParams(vmem_limit_bytes=24 << 20),
        cost_estimate=pl.CostEstimate(
            flops=40 * count * width_x * groups * width_y,
            bytes_accessed=8 * count * width_x * groups * width_y,
            transcendentals=0,
        ),
        name="transport_first",
    )(tracers, wind_x, wind_y, table)


def second_part(
    state, left, right, wind_x, wind_y, wind_l, wind_r, table, mean, start
):
    count, width_x, groups, width_y = state.shape
    step = 3
    skip = start // step
    spec_s = pl.BlockSpec((step, width_x, groups, width_y), lambda i: (i, 0, 0, 0))
    spec_m = pl.BlockSpec((step, 2, groups, width_y), lambda i: (i, 0, 0, 0))
    spec_w = pl.BlockSpec((step, width_x, width_y), lambda i: (i + skip, 0, 0))
    spec_n = pl.BlockSpec((step, 2, width_y), lambda i: (i + skip, 0, 0))
    return pl.pallas_call(
        lambda *refs: second_kernel(step, *refs),
        grid=(count // step,),
        in_specs=[
            spec_s, spec_m, spec_m, spec_w, spec_w, spec_n, spec_n,
            pl.BlockSpec(table.shape, lambda i: (0, 0)),
            pl.BlockSpec(mean.shape, lambda i: (0, 0)),
        ],
        out_specs=pl.BlockSpec(
            (step, len(TRIPLES), width_y, LANES), lambda i: (i, 0, 0, 0)
        ),
        out_shape=jax.ShapeDtypeStruct((count, len(TRIPLES), width_y, LANES), BF16),
        compiler_params=pltpu.CompilerParams(vmem_limit_bytes=24 << 20),
        cost_estimate=pl.CostEstimate(
            flops=40 * count * width_x * groups * width_y,
            bytes_accessed=8 * count * width_x * groups * width_y,
            transcendentals=0,
        ),
        name="transport_second",
    )(state, left, right, wind_x, wind_y, wind_l, wind_r, table, mean)


def solve_kernel(n_fields, n_pieces, pos_ref, *refs):
    fields = refs[:n_fields]
    pieces = refs[n_fields : n_fields + n_pieces]
    out_ref = refs[n_fields + n_pieces]
    matrices, value, result, final = refs[n_fields + n_pieces + 1 :]
    groups, rows, width_x, width_y = out_ref.shape
    levels = value.shape[0] // width_y
    per_block = pieces[0].shape[2] // levels

    base = 0
    for piece in pieces:
        count = piece.shape[0]

        @pl.loop(0, count)
        def _(k, piece=piece, base=base):
            for j in range(per_block):
                tile, shift = divmod(j * levels, LANES)
                part = piece[k, :, tile * LANES : (tile + 1) * LANES].astype(F32)
                if shift:
                    part = pltpu.roll(part, LANES - shift, axis=1)
                if shift + levels > LANES:
                    after = piece[k, :, (tile + 1) * LANES : (tile + 2) * LANES].astype(F32)
                    after = pltpu.roll(after, LANES - shift, axis=1)
                    lane = lax.broadcasted_iota(jnp.int32, after.shape, 1)
                    part = jnp.where(lane < LANES - shift, part, after)
                matrices[(base + k) * per_block + j, : part.shape[0]] = part.astype(BF16)

        base += count

    lane = lax.broadcasted_iota(jnp.int32, (rows, LANES), 1)
    eye = (
        lax.broadcasted_iota(jnp.int32, (LANES, LANES), 0)
        == lax.broadcasted_iota(jnp.int32, (LANES, LANES), 1)
    ).astype(F32).astype(BF16)
    for g, triple in enumerate(TRIPLES):
        level = 0
        for field in fields:
            for l in range(field.shape[0]):
                value[pl.ds(level, width_y, stride=levels), :] = field[l, g].astype(F32)
                level += 1

        @pl.loop(0, width_y, unroll=16)
        def _(y, triple=triple):
            start = pl.multiple_of(y * levels, 8)
            columns = value[pl.ds(start, levels), :]
            columns = jnp.concatenate(
                [columns, jnp.zeros((LANES - levels, LANES), F32)], axis=0
            ).astype(BF16)
            chosen = jnp.concatenate([matrices[pos_ref[x, y]] for x in triple], axis=0)
            product = jnp.dot(chosen, columns, preferred_element_type=F32)
            picked = product[(len(triple) - 1) * HEIGHT :][:rows]
            for i in range(len(triple) - 2, -1, -1):
                picked = jnp.where(
                    lane < (i + 1) * groups, product[i * HEIGHT : i * HEIGHT + rows], picked
                )
            result[pl.ds(y, rows, stride=width_y), :] = picked

        @pl.loop(0, rows, unroll=12)
        def _(a, triple=triple):
            start = pl.multiple_of(a * width_y, width_y)
            solved = result[pl.ds(start, width_y), :].astype(BF16)
            turned = lax.dot_general(
                eye, solved, (((1,), (1,)), ((), ())), preferred_element_type=F32
            )
            for i, x in enumerate(triple):
                final[a, pl.ds(x, groups, stride=width_x), :] = turned[
                    i * groups : (i + 1) * groups
                ]

    @pl.loop(0, rows, unroll=4)
    def _(a):
        out_ref[:, a] = final[a].reshape(groups, width_x, width_y).astype(BF16)


def solve(fields, pieces, position, groups, levels_out, width_x, width_y):
    levels = sum(f.shape[0] for f in fields)
    spans = sum(p.shape[0] * p.shape[2] for p in pieces) // levels
    vmem = pl.BlockSpec(memory_space=pltpu.VMEM)
    return pl.pallas_call(
        functools.partial(solve_kernel, len(fields), len(pieces)),
        in_specs=[pl.BlockSpec(memory_space=pltpu.SMEM)]
        + [vmem] * (len(fields) + len(pieces)),
        out_specs=vmem,
        out_shape=jax.ShapeDtypeStruct((groups, levels_out, width_x, width_y), BF16),
        scratch_shapes=[
            pltpu.VMEM((spans, HEIGHT, LANES), BF16),
            pltpu.VMEM((width_y * levels, LANES), F32),
            pltpu.VMEM((levels_out * width_y, LANES), F32),
            pltpu.VMEM((levels_out, groups * width_x, width_y), F32),
        ],
        compiler_params=pltpu.CompilerParams(vmem_limit_bytes=52 << 20),
        cost_estimate=pl.CostEstimate(
            flops=2 * levels_out * levels * groups * width_x * width_y,
            bytes_accessed=12 << 20,
            transcendentals=0,
        ),
        name="solve_columns",
    )(position, *fields, *pieces)


def elem_index(y, x, z):
    return (y % NY_CHIPS * NX_CHIPS + x % NX_CHIPS) * NZ_CHIPS + z % NZ_CHIPS


def fetch(value, dy=0, dx=0, dz=0):
    pairs = [
        (elem_index(y + dy, x + dx, z + dz), elem_index(y, x, z))
        for y in range(NY_CHIPS)
        for x in range(NX_CHIPS)
        for z in range(NZ_CHIPS)
    ]
    return lax.ppermute(value, ELEM, pairs)


def gather_matrices(block):
    near = [block] + [fetch(block, dz=d) for d in range(1, NZ_CHIPS)]
    part = jnp.concatenate(near, axis=1)
    return [lax.all_gather(part, ("y", "x"), axis=0)]


def span_position(span_ids, per_dev):
    owner, local = span_ids // per_dev, span_ids % per_dev
    dz = (owner % NZ_CHIPS - lax.axis_index("z")) % NZ_CHIPS
    return (owner // NZ_CHIPS * NZ_CHIPS + dz) * per_dev + local


def body(tracers, wind_x, wind_y, span_of, inverses):
    groups, half_levels, width_x, width_y = tracers.shape
    per_dev = inverses.shape[0]
    first_table, second_table, mean = table_y(width_y)
    size = NY_CHIPS * NX_CHIPS * NZ_CHIPS
    up = [(i, (i + 1) % size) for i in range(size)]
    down = [(j, i) for i, j in up]
    lev = lax.axis_index("lev")

    mine = lax.dynamic_slice_in_dim(inverses, lev * half_levels, half_levels, 1)
    own = lax.dynamic_slice_in_dim(mine, lev * half_levels, half_levels, 2)
    other = lax.dynamic_slice_in_dim(mine, (1 - lev) * half_levels, half_levels, 2)
    block = jnp.concatenate([own, other], axis=2).transpose(1, 0, 2)
    block = block.reshape(half_levels, -1)
    block = jnp.pad(block, ((0, -half_levels % 8), (0, 0)))
    pieces = gather_matrices(block)
    position = span_position(span_of[:, 0], per_dev).reshape(width_x, width_y)

    wind_l = lax.ppermute(jnp.stack([wind_x[:, -1], wind_y[:, -1]], 1), ELEM, up)
    wind_r = lax.ppermute(jnp.stack([wind_x[:, 0], wind_y[:, 0]], 1), ELEM, down)

    count = half_levels // CHUNKS
    firsts = [
        first_part(tracers, wind_x, wind_y, first_table, i * count, count)
        for i in range(CHUNKS)
    ]
    own_fields, other_fields = [], []
    for i, (state, to_left, to_right) in enumerate(firsts):
        left = lax.ppermute(to_right, ELEM, up)
        right = lax.ppermute(to_left, ELEM, down)
        field = second_part(
            state, left, right, wind_x, wind_y, wind_l, wind_r, second_table, mean, i * count
        )
        own_fields.append(field)
        other_fields.append(lax.ppermute(field, "lev", [(0, 1), (1, 0)]))
    return solve(
        own_fields + other_fields, pieces, position, groups, half_levels, width_x, width_y
    )


def solution(mesh):
    chips = jax.sharding.Mesh(
        mesh.devices.reshape(NY_CHIPS, NX_CHIPS, NZ_CHIPS, -1), ELEM + ("lev",)
    )
    return jax.shard_map(
        body,
        mesh=chips,
        in_specs=(
            P(None, "lev", ELEM, None),
            P("lev", ELEM, None),
            P("lev", ELEM, None),
            P(ELEM, None),
            P(ELEM, None, None),
        ),
        out_specs=P(None, "lev", ELEM, None),
        check_vma=False,
    )
```

```python
import functools

import jax
import jax.numpy as jnp
import numpy as np
from jax import lax
from jax.experimental import pallas as pl
from jax.experimental.pallas import tpu as pltpu
from jax.sharding import PartitionSpec as P

NP = 4
TIME_STEP = 0.08
NY_CHIPS, NX_CHIPS, NZ_CHIPS = 4, 4, 8
ELEM = ("y", "x", "z")
CHUNKS = 2
LANES = 128
TRIPLES = ((0, 1, 2), (3, 4, 5), (6, 7))
HEIGHT = 48
DEPTH = 80
F32, BF16 = jnp.float32, jnp.bfloat16


def derivative_table():
    nodes = np.array([-1.0, -1.0 / np.sqrt(5.0), 1.0 / np.sqrt(5.0), 1.0])
    table = np.zeros((NP, NP))
    for i in range(NP):
        for k in range(NP):
            if i == k:
                table[i, k] = sum(1.0 / (nodes[i] - nodes[m]) for m in range(NP) if m != i)
            else:
                top = np.prod([nodes[i] - nodes[m] for m in range(NP) if m != k and m != i])
                table[i, k] = top / np.prod([nodes[k] - nodes[m] for m in range(NP) if m != k])
    return table


D = derivative_table()
D = [[float(D[i, k]) for k in range(NP)] for i in range(NP)]


def table_y(width):
    full = np.kron(np.eye(width // NP), np.array(D)).T.astype(np.float32)
    hi = full.astype(jnp.bfloat16)
    lo = (full - hi.astype(np.float32)).astype(jnp.bfloat16)
    first = np.concatenate([hi, lo], axis=0)
    zero = np.zeros_like(lo)
    second = np.concatenate(
        [np.concatenate([hi, lo], axis=1), np.concatenate([hi, zero], axis=1)], axis=0
    )
    mean = np.eye(width)
    for y in range(width):
        if y % NP in (0, NP - 1):
            mean[y, y] = mean[y, (y + (1 if y % NP else -1)) % width] = 0.5
    mean = np.concatenate([mean, mean], axis=1).astype(jnp.bfloat16)
    return jnp.asarray(first), jnp.asarray(second), jnp.asarray(mean)


def grad_x(s0, s1, s2, s3):
    m, n = s3 - s0, s2 - s1
    e = (s0 + s3) - (s1 + s2)
    a = 0.5 * (D[3][3] + D[0][3])
    b = 0.5 * (D[0][1] + D[3][1])
    u = a * m - b * n
    v = (0.5 * (D[1][3] + D[2][3])) * m + (0.5 * (D[1][2] + D[2][2])) * n
    w = (0.5 * (D[3][3] - D[0][3])) * e
    z = (0.5 * (D[2][3] - D[1][3])) * e
    return [u - w, v - z, v + z, u + w]


def mean_y(value, last, inner):
    width = value.shape[1]
    ahead = pltpu.roll(value, width - 1, axis=1)
    behind = pltpu.roll(value, 1, axis=1)
    return jnp.where(inner, value, 0.5 * (value + jnp.where(last, ahead, behind)))


def node_masks(shape):
    node = lax.broadcasted_iota(jnp.int32, shape, 1) % NP
    return node == NP - 1, (node == 1) | (node == 2)


def first_kernel(levels, t_ref, wx_ref, wy_ref, d_ref, st_ref, dn_ref, up_ref, scr):
    groups, width_x, width_y = t_ref.shape[0], t_ref.shape[2], t_ref.shape[3]
    last, inner = node_masks((groups, width_y))

    @pl.loop(0, levels, unroll=3)
    def _(l):
        scr[...] = t_ref[:, l].astype(F32).reshape(groups * width_x, width_y)
        s = [scr[pl.ds(x, groups, stride=width_x), :] for x in range(width_x)]
        wx = wx_ref[l].astype(F32) * TIME_STEP
        wy = wy_ref[l].astype(F32) * TIME_STEP
        flat = jnp.concatenate(s, axis=0).astype(BF16)
        gy = jnp.dot(
            jnp.concatenate([flat, flat], axis=1), d_ref[...], preferred_element_type=F32
        )
        gx = grad_x(*s[:4]) + grad_x(*s[4:])
        adv = [
            s[x]
            - (wx[x : x + 1] * gx[x] + wy[x : x + 1] * gy[x * groups : (x + 1) * groups])
            for x in range(width_x)
        ]
        middle = mean_y(0.5 * (adv[3] + adv[4]), last, inner)
        st = [adv[0], None, None, middle, middle, None, None, adv[7]]
        for x in (1, 2, 5, 6):
            st[x] = mean_y(adv[x], last, inner)
        for x in range(width_x):
            st_ref[l, x] = st[x]
        part = D[0][1] * st[1] + D[0][2] * st[2] + D[0][3] * st[3]
        dn_ref[l, 0] = adv[0].astype(BF16)
        dn_ref[l, 1] = (-wx[0:1] * part).astype(BF16)
        part = D[3][0] * st[4] + D[3][1] * st[5] + D[3][2] * st[6]
        up_ref[l, 0] = adv[7].astype(BF16)
        up_ref[l, 1] = (-wx[7:8] * part).astype(BF16)


def second_kernel(
    levels, st_ref, left_ref, right_ref, wx_ref, wy_ref, wl_ref, wr_ref, d_ref, m_ref, out_ref
):
    width_x, groups, width_y = st_ref.shape[1:]
    last, inner = node_masks((groups, width_y))

    @pl.loop(0, levels, unroll=3)
    def _(l):
        s = [None] + [st_ref[l, x] for x in range(1, 7)] + [None]
        s[0] = mean_y(0.5 * (st_ref[l, 0] + left_ref[l, 0].astype(F32)), last, inner)
        s[7] = mean_y(0.5 * (st_ref[l, 7] + right_ref[l, 0].astype(F32)), last, inner)
        wx = wx_ref[l].astype(F32) * TIME_STEP
        wy = wy_ref[l].astype(F32) * TIME_STEP
        wl = wl_ref[l].astype(F32) * TIME_STEP
        wr = wr_ref[l].astype(F32) * TIME_STEP
        flat = jnp.concatenate(s, axis=0)
        hi = flat.astype(BF16)
        lo = (flat - hi.astype(F32)).astype(BF16)
        both = jnp.dot(
            jnp.concatenate([hi, lo], axis=1), d_ref[...], preferred_element_type=F32
        )
        gy = both[:, :width_y] + both[:, width_y:]
        gys = [gy[x * groups : (x + 1) * groups] for x in range(width_x)]
        gx = grad_x(*s[:4]) + grad_x(*s[4:])
        adv = [
            s[x] - (wx[x : x + 1] * gx[x] + wy[x : x + 1] * gys[x]) for x in range(width_x)
        ]
        before = (
            s[0]
            - ((wl[0:1] * D[3][3]) * s[0] + wl[1:2] * gys[0])
            + left_ref[l, 1].astype(F32)
        )
        after = (
            s[7]
            - ((wr[0:1] * D[0][0]) * s[7] + wr[1:2] * gys[7])
            + right_ref[l, 1].astype(F32)
        )
        middle = 0.5 * (adv[3] + adv[4])
        adv[0] = 0.5 * (before + adv[0])
        adv[7] = 0.5 * (adv[7] + after)
        adv[3] = adv[4] = middle
        for g, triple in enumerate(TRIPLES):
            rest = jnp.zeros((LANES - len(triple) * groups, width_y), F32)
            flat = jnp.concatenate([adv[x] for x in triple] + [rest], axis=0)
            hi = flat.astype(BF16)
            lo = (flat - hi.astype(F32)).astype(BF16)
            out_ref[l, g] = lax.dot_general(
                m_ref[...],
                jnp.concatenate([hi, lo], axis=1),
                (((1,), (1,)), ((), ())),
                preferred_element_type=F32,
            ).astype(BF16)


def first_part(tracers, wind_x, wind_y, table, start, count):
    groups, _, width_x, width_y = tracers.shape
    step = 3
    skip = start // step
    spec_w = pl.BlockSpec((step, width_x, width_y), lambda i: (i + skip, 0, 0))
    spec_m = pl.BlockSpec((step, 2, groups, width_y), lambda i: (i, 0, 0, 0))
    return pl.pallas_call(
        lambda *refs: first_kernel(step, *refs),
        grid=(count // step,),
        in_specs=[
            pl.BlockSpec((groups, step, width_x, width_y), lambda i: (0, i + skip, 0, 0)),
            spec_w,
            spec_w,
            pl.BlockSpec(table.shape, lambda i: (0, 0)),
        ],
        out_specs=[
            pl.BlockSpec((step, width_x, groups, width_y), lambda i: (i, 0, 0, 0)),
            spec_m,
            spec_m,
        ],
        out_shape=[
            jax.ShapeDtypeStruct((count, width_x, groups, width_y), F32),
            jax.ShapeDtypeStruct((count, 2, groups, width_y), BF16),
            jax.ShapeDtypeStruct((count, 2, groups, width_y), BF16),
        ],
        scratch_shapes=[pltpu.VMEM((groups * width_x, width_y), F32)],
        compiler_params=pltpu.CompilerParams(vmem_limit_bytes=24 << 20),
        cost_estimate=pl.CostEstimate(
            flops=40 * count * width_x * groups * width_y,
            bytes_accessed=8 * count * width_x * groups * width_y,
            transcendentals=0,
        ),
        name="transport_first",
    )(tracers, wind_x, wind_y, table)


def second_part(
    state, left, right, wind_x, wind_y, wind_l, wind_r, table, mean, start
):
    count, width_x, groups, width_y = state.shape
    step = 3
    skip = start // step
    spec_s = pl.BlockSpec((step, width_x, groups, width_y), lambda i: (i, 0, 0, 0))
    spec_m = pl.BlockSpec((step, 2, groups, width_y), lambda i: (i, 0, 0, 0))
    spec_w = pl.BlockSpec((step, width_x, width_y), lambda i: (i + skip, 0, 0))
    spec_n = pl.BlockSpec((step, 2, width_y), lambda i: (i + skip, 0, 0))
    return pl.pallas_call(
        lambda *refs: second_kernel(step, *refs),
        grid=(count // step,),
        in_specs=[
            spec_s, spec_m, spec_m, spec_w, spec_w, spec_n, spec_n,
            pl.BlockSpec(table.shape, lambda i: (0, 0)),
            pl.BlockSpec(mean.shape, lambda i: (0, 0)),
        ],
        out_specs=pl.BlockSpec(
            (step, len(TRIPLES), width_y, LANES), lambda i: (i, 0, 0, 0)
        ),
        out_shape=jax.ShapeDtypeStruct((count, len(TRIPLES), width_y, LANES), BF16),
        compiler_params=pltpu.CompilerParams(vmem_limit_bytes=24 << 20),
        cost_estimate=pl.CostEstimate(
            flops=40 * count * width_x * groups * width_y,
            bytes_accessed=8 * count * width_x * groups * width_y,
            transcendentals=0,
        ),
        name="transport_second",
    )(state, left, right, wind_x, wind_y, wind_l, wind_r, table, mean)


def align_kernel(n_fields, *refs):
    fields, out_ref, scratch = refs[:n_fields], refs[n_fields], refs[n_fields + 1]
    width_y = fields[0].shape[2]
    level = 0
    for field in fields:
        for l in range(field.shape[0]):
            scratch[pl.ds(level, width_y, stride=DEPTH), :] = field[l, 0].astype(F32)
            level += 1
    for l in range(level, DEPTH):
        scratch[pl.ds(l, width_y, stride=DEPTH), :] = jnp.zeros((width_y, LANES), F32)

    @pl.loop(0, width_y, unroll=8)
    def _(y):
        rows = pl.ds(pl.multiple_of(y * DEPTH, DEPTH), DEPTH)
        out_ref[0, rows, :] = scratch[rows, :].astype(BF16)


def align(fields):
    _, triples, width_y, lanes = fields[0].shape
    return pl.pallas_call(
        functools.partial(align_kernel, len(fields)),
        grid=(triples,),
        in_specs=[
            pl.BlockSpec((f.shape[0], 1, width_y, lanes), lambda g: (0, g, 0, 0)) for f in fields
        ],
        out_specs=pl.BlockSpec((1, width_y * DEPTH, lanes), lambda g: (g, 0, 0)),
        out_shape=jax.ShapeDtypeStruct((triples, width_y * DEPTH, lanes), BF16),
        scratch_shapes=[pltpu.VMEM((width_y * DEPTH, lanes), F32)],
        compiler_params=pltpu.CompilerParams(vmem_limit_bytes=24 << 20),
        cost_estimate=pl.CostEstimate(flops=1000, bytes_accessed=1000, transcendentals=0),
        name="align_columns",
    )(*fields)


def lanes_from(ref, k, rows, start):
    tile, shift = divmod(start, LANES)
    part = ref[k, rows, tile * LANES : (tile + 1) * LANES].astype(F32)
    if shift:
        part = pltpu.roll(part, LANES - shift, axis=1)
        if (tile + 2) * LANES <= ref.shape[2]:
            after = ref[k, rows, (tile + 1) * LANES : (tile + 2) * LANES].astype(F32)
            after = pltpu.roll(after, LANES - shift, axis=1)
            lane = lax.broadcasted_iota(jnp.int32, part.shape, 1)
            part = jnp.where(lane < LANES - shift, part, after)
    return part


def solve_kernel(
    pos_ref, value_hbm, block_hbm, out_ref,
    value_ref, block_ref, matrices, result, final, value_sem, block_sem,
):
    groups, rows, width_x, width_y = out_ref.shape
    levels = 2 * rows

    count, _, lanes = block_ref.shape

    def block_copy(k):
        return pltpu.make_async_copy(block_hbm.at[k], block_ref.at[k], block_sem.at[k])

    for k in range(count):
        block_copy(k).start()
    value_copy = pltpu.make_async_copy(value_hbm, value_ref, value_sem)
    value_copy.start()
    per_block = lanes // levels
    tall = -(-rows // 8) * 8

    @pl.loop(0, count)
    def _(k):
        block_copy(k).wait()
        for j in range(per_block):
            part = lanes_from(block_ref, k, slice(0, tall), j * levels)
            matrices[2 * k * per_block + j, :tall] = part.astype(BF16)
            part = lanes_from(block_ref, k, slice(2 * rows - tall, 2 * rows), j * levels)
            part = pltpu.roll(part, rows, axis=0)
            matrices[(2 * k + 1) * per_block + j, :tall] = part.astype(BF16)

    value_copy.wait()
    lane = lax.broadcasted_iota(jnp.int32, (rows, LANES), 1)
    eye = (
        lax.broadcasted_iota(jnp.int32, (LANES, LANES), 0)
        == lax.broadcasted_iota(jnp.int32, (LANES, LANES), 1)
    ).astype(F32).astype(BF16)
    for g, triple in enumerate(TRIPLES):

        @pl.loop(0, width_y, unroll=16)
        def _(y, g=g, triple=triple):
            columns = value_ref[g, pl.ds(pl.multiple_of(y * DEPTH, DEPTH), DEPTH), :]
            columns = jnp.concatenate(
                [columns, jnp.zeros((LANES - DEPTH, LANES), BF16)], axis=0
            )
            chosen = jnp.concatenate([matrices[pos_ref[x, y]] for x in triple], axis=0)
            product = jnp.dot(chosen, columns, preferred_element_type=F32)
            picked = product[(len(triple) - 1) * HEIGHT :][:rows]
            for i in range(len(triple) - 2, -1, -1):
                picked = jnp.where(
                    lane < (i + 1) * groups, product[i * HEIGHT : i * HEIGHT + rows], picked
                )
            result[pl.ds(y, rows, stride=width_y), :] = picked

        @pl.loop(0, rows, unroll=12)
        def _(a, triple=triple):
            start = pl.multiple_of(a * width_y, width_y)
            turned = lax.dot_general(
                eye,
                result[pl.ds(start, width_y), :].astype(BF16),
                (((1,), (1,)), ((), ())),
                preferred_element_type=F32,
            )
            for i, x in enumerate(triple):
                final[a, pl.ds(x, groups, stride=width_x), :] = turned[
                    i * groups : (i + 1) * groups
                ]

    @pl.loop(0, rows, unroll=4)
    def _(a):
        out_ref[:, a] = final[a].reshape(groups, width_x, width_y).astype(BF16)


def solve(value, block, position, shape):
    groups, rows, width_x, width_y = shape
    spans = 2 * block.shape[0] * (block.shape[2] // (2 * rows))
    anywhere = pl.BlockSpec(memory_space=pl.ANY)
    return pl.pallas_call(
        solve_kernel,
        in_specs=[pl.BlockSpec(memory_space=pltpu.SMEM), anywhere, anywhere],
        out_specs=pl.BlockSpec(memory_space=pltpu.VMEM),
        out_shape=jax.ShapeDtypeStruct(shape, BF16),
        scratch_shapes=[
            pltpu.VMEM(value.shape, BF16),
            pltpu.VMEM(block.shape, BF16),
            pltpu.VMEM((spans, HEIGHT, LANES), BF16),
            pltpu.VMEM((rows * width_y, LANES), F32),
            pltpu.VMEM((rows, groups * width_x, width_y), F32),
            pltpu.SemaphoreType.DMA(()),
            pltpu.SemaphoreType.DMA((block.shape[0],)),
        ],
        compiler_params=pltpu.CompilerParams(vmem_limit_bytes=58 << 20),
        cost_estimate=pl.CostEstimate(
            flops=4 * rows * rows * groups * width_x * width_y,
            bytes_accessed=12 << 20,
            transcendentals=0,
        ),
        name="solve_columns",
    )(position, value, block)


def elem_index(y, x, z):
    return (y % NY_CHIPS * NX_CHIPS + x % NX_CHIPS) * NZ_CHIPS + z % NZ_CHIPS


def fetch(value, dy=0, dx=0, dz=0):
    pairs = [
        (elem_index(y + dy, x + dx, z + dz), elem_index(y, x, z))
        for y in range(NY_CHIPS)
        for x in range(NX_CHIPS)
        for z in range(NZ_CHIPS)
    ]
    return lax.ppermute(value, ELEM, pairs)


def gather_matrices(block):
    near = [block] + [fetch(block, dz=d) for d in range(1, NZ_CHIPS)]
    half = NZ_CHIPS // 2
    halves = [jnp.concatenate(near[i : i + half], axis=1) for i in (0, half)]
    return lax.all_gather(jnp.concatenate(halves, axis=0), ("y", "x"), axis=0)


def span_position(span_ids, per_dev):
    owner, local = span_ids // per_dev, span_ids % per_dev
    dz = (owner % NZ_CHIPS - lax.axis_index("z")) % NZ_CHIPS
    return (owner // NZ_CHIPS * NZ_CHIPS + dz) * per_dev + local


def body(tracers, wind_x, wind_y, span_of, inverses):
    groups, half_levels, width_x, width_y = tracers.shape
    per_dev = inverses.shape[0]
    first_table, second_table, mean = table_y(width_y)
    size = NY_CHIPS * NX_CHIPS * NZ_CHIPS
    up = [(i, (i + 1) % size) for i in range(size)]
    down = [(j, i) for i, j in up]
    lev = lax.axis_index("lev")

    mine = lax.dynamic_slice_in_dim(inverses, lev * half_levels, half_levels, 1)
    own = lax.dynamic_slice_in_dim(mine, lev * half_levels, half_levels, 2)
    other = lax.dynamic_slice_in_dim(mine, (1 - lev) * half_levels, half_levels, 2)
    block = jnp.concatenate([own, other], axis=2).transpose(1, 0, 2)
    block = block.reshape(half_levels, -1)
    matrices = gather_matrices(block)
    position = span_position(span_of[:, 0], per_dev).reshape(width_x, width_y)

    wind_l = lax.ppermute(jnp.stack([wind_x[:, -1], wind_y[:, -1]], 1), ELEM, up)
    wind_r = lax.ppermute(jnp.stack([wind_x[:, 0], wind_y[:, 0]], 1), ELEM, down)

    count = half_levels // CHUNKS
    firsts = [
        first_part(tracers, wind_x, wind_y, first_table, i * count, count)
        for i in range(CHUNKS)
    ]
    own_fields, other_fields = [], []
    for i, (state, to_left, to_right) in enumerate(firsts):
        left = lax.ppermute(to_right, ELEM, up)
        right = lax.ppermute(to_left, ELEM, down)
        field = second_part(
            state, left, right, wind_x, wind_y, wind_l, wind_r, second_table, mean, i * count
        )
        own_fields.append(field)
        other_fields.append(lax.ppermute(field, "lev", [(0, 1), (1, 0)]))
    value = align(own_fields + other_fields)
    return solve(value, matrices, position, tracers.shape)


def solution(mesh):
    chips = jax.sharding.Mesh(
        mesh.devices.reshape(NY_CHIPS, NX_CHIPS, NZ_CHIPS, -1), ELEM + ("lev",)
    )
    return jax.shard_map(
        body,
        mesh=chips,
        in_specs=(
            P(None, "lev", ELEM, None),
            P("lev", ELEM, None),
            P("lev", ELEM, None),
            P(ELEM, None),
            P(ELEM, None, None),
        ),
        out_specs=P(None, "lev", ELEM, None),
        check_vma=False,
    )
```

```python
import functools

import jax
import jax.numpy as jnp
import numpy as np
from jax import lax
from jax.experimental import pallas as pl
from jax.experimental.pallas import tpu as pltpu
from jax.sharding import PartitionSpec as P

NP = 4
TIME_STEP = 0.08
NY_CHIPS, NX_CHIPS, NZ_CHIPS = 4, 4, 8
ELEM = ("y", "x", "z")
CHUNKS = 2
LANES = 128
TRIPLES = ((0, 1, 2), (3, 4, 5), (6, 7))
HEIGHT = 48
DEPTH = 80
F32, BF16 = jnp.float32, jnp.bfloat16


def derivative_table():
    nodes = np.array([-1.0, -1.0 / np.sqrt(5.0), 1.0 / np.sqrt(5.0), 1.0])
    table = np.zeros((NP, NP))
    for i in range(NP):
        for k in range(NP):
            if i == k:
                table[i, k] = sum(1.0 / (nodes[i] - nodes[m]) for m in range(NP) if m != i)
            else:
                top = np.prod([nodes[i] - nodes[m] for m in range(NP) if m != k and m != i])
                table[i, k] = top / np.prod([nodes[k] - nodes[m] for m in range(NP) if m != k])
    return table


D = derivative_table()
D = [[float(D[i, k]) for k in range(NP)] for i in range(NP)]


def table_y(width):
    full = np.kron(np.eye(width // NP), np.array(D)).T.astype(np.float32)
    hi = full.astype(jnp.bfloat16)
    lo = (full - hi.astype(np.float32)).astype(jnp.bfloat16)
    first = np.concatenate([hi, lo], axis=0)
    zero = np.zeros_like(lo)
    second = np.concatenate(
        [np.concatenate([hi, lo], axis=1), np.concatenate([hi, zero], axis=1)], axis=0
    )
    mean = np.eye(width)
    for y in range(width):
        if y % NP in (0, NP - 1):
            mean[y, y] = mean[y, (y + (1 if y % NP else -1)) % width] = 0.5
    mean = np.concatenate([mean, mean], axis=1).astype(jnp.bfloat16)
    return jnp.asarray(first), jnp.asarray(second), jnp.asarray(mean)


def grad_x(s0, s1, s2, s3):
    m, n = s3 - s0, s2 - s1
    e = (s0 + s3) - (s1 + s2)
    a = 0.5 * (D[3][3] + D[0][3])
    b = 0.5 * (D[0][1] + D[3][1])
    u = a * m - b * n
    v = (0.5 * (D[1][3] + D[2][3])) * m + (0.5 * (D[1][2] + D[2][2])) * n
    w = (0.5 * (D[3][3] - D[0][3])) * e
    z = (0.5 * (D[2][3] - D[1][3])) * e
    return [u - w, v - z, v + z, u + w]


def mean_y(value, last, inner):
    width = value.shape[1]
    ahead = pltpu.roll(value, width - 1, axis=1)
    behind = pltpu.roll(value, 1, axis=1)
    return jnp.where(inner, value, 0.5 * (value + jnp.where(last, ahead, behind)))


def node_masks(shape):
    node = lax.broadcasted_iota(jnp.int32, shape, 1) % NP
    return node == NP - 1, (node == 1) | (node == 2)


def first_kernel(levels, t_ref, wx_ref, wy_ref, d_ref, st_ref, dn_ref, up_ref, scr):
    groups, width_x, width_y = t_ref.shape[0], t_ref.shape[2], t_ref.shape[3]
    last, inner = node_masks((groups, width_y))

    @pl.loop(0, levels, unroll=3)
    def _(l):
        scr[...] = t_ref[:, l].astype(F32).reshape(groups * width_x, width_y)
        s = [scr[pl.ds(x, groups, stride=width_x), :] for x in range(width_x)]
        wx = wx_ref[l].astype(F32) * TIME_STEP
        wy = wy_ref[l].astype(F32) * TIME_STEP
        flat = jnp.concatenate(s, axis=0).astype(BF16)
        gy = jnp.dot(
            jnp.concatenate([flat, flat], axis=1), d_ref[...], preferred_element_type=F32
        )
        gx = grad_x(*s[:4]) + grad_x(*s[4:])
        adv = [
            s[x]
            - (wx[x : x + 1] * gx[x] + wy[x : x + 1] * gy[x * groups : (x + 1) * groups])
            for x in range(width_x)
        ]
        middle = mean_y(0.5 * (adv[3] + adv[4]), last, inner)
        st = [adv[0], None, None, middle, middle, None, None, adv[7]]
        for x in (1, 2, 5, 6):
            st[x] = mean_y(adv[x], last, inner)
        for x in range(width_x):
            st_ref[l, x] = st[x]
        part = D[0][1] * st[1] + D[0][2] * st[2] + D[0][3] * st[3]
        dn_ref[l, 0] = adv[0].astype(BF16)
        dn_ref[l, 1] = (-wx[0:1] * part).astype(BF16)
        part = D[3][0] * st[4] + D[3][1] * st[5] + D[3][2] * st[6]
        up_ref[l, 0] = adv[7].astype(BF16)
        up_ref[l, 1] = (-wx[7:8] * part).astype(BF16)


def second_kernel(
    levels, st_ref, left_ref, right_ref, wx_ref, wy_ref, wl_ref, wr_ref, d_ref, m_ref, out_ref
):
    width_x, groups, width_y = st_ref.shape[1:]
    last, inner = node_masks((groups, width_y))

    @pl.loop(0, levels, unroll=3)
    def _(l):
        s = [None] + [st_ref[l, x] for x in range(1, 7)] + [None]
        s[0] = mean_y(0.5 * (st_ref[l, 0] + left_ref[l, 0].astype(F32)), last, inner)
        s[7] = mean_y(0.5 * (st_ref[l, 7] + right_ref[l, 0].astype(F32)), last, inner)
        wx = wx_ref[l].astype(F32) * TIME_STEP
        wy = wy_ref[l].astype(F32) * TIME_STEP
        wl = wl_ref[l].astype(F32) * TIME_STEP
        wr = wr_ref[l].astype(F32) * TIME_STEP
        flat = jnp.concatenate(s, axis=0)
        hi = flat.astype(BF16)
        lo = (flat - hi.astype(F32)).astype(BF16)
        both = jnp.dot(
            jnp.concatenate([hi, lo], axis=1), d_ref[...], preferred_element_type=F32
        )
        gy = both[:, :width_y] + both[:, width_y:]
        gys = [gy[x * groups : (x + 1) * groups] for x in range(width_x)]
        gx = grad_x(*s[:4]) + grad_x(*s[4:])
        adv = [
            s[x] - (wx[x : x + 1] * gx[x] + wy[x : x + 1] * gys[x]) for x in range(width_x)
        ]
        before = (
            s[0]
            - ((wl[0:1] * D[3][3]) * s[0] + wl[1:2] * gys[0])
            + left_ref[l, 1].astype(F32)
        )
        after = (
            s[7]
            - ((wr[0:1] * D[0][0]) * s[7] + wr[1:2] * gys[7])
            + right_ref[l, 1].astype(F32)
        )
        middle = 0.5 * (adv[3] + adv[4])
        adv[0] = 0.5 * (before + adv[0])
        adv[7] = 0.5 * (adv[7] + after)
        adv[3] = adv[4] = middle
        for g, triple in enumerate(TRIPLES):
            rest = jnp.zeros((LANES - len(triple) * groups, width_y), F32)
            flat = jnp.concatenate([adv[x] for x in triple] + [rest], axis=0)
            hi = flat.astype(BF16)
            lo = (flat - hi.astype(F32)).astype(BF16)
            out_ref[l, g] = lax.dot_general(
                m_ref[...],
                jnp.concatenate([hi, lo], axis=1),
                (((1,), (1,)), ((), ())),
                preferred_element_type=F32,
            ).astype(BF16)


def first_part(tracers, wind_x, wind_y, table, start, count):
    groups, _, width_x, width_y = tracers.shape
    step = 3
    skip = start // step
    spec_w = pl.BlockSpec((step, width_x, width_y), lambda i: (i + skip, 0, 0))
    spec_m = pl.BlockSpec((step, 2, groups, width_y), lambda i: (i, 0, 0, 0))
    return pl.pallas_call(
        lambda *refs: first_kernel(step, *refs),
        grid=(count // step,),
        in_specs=[
            pl.BlockSpec((groups, step, width_x, width_y), lambda i: (0, i + skip, 0, 0)),
            spec_w,
            spec_w,
            pl.BlockSpec(table.shape, lambda i: (0, 0)),
        ],
        out_specs=[
            pl.BlockSpec((step, width_x, groups, width_y), lambda i: (i, 0, 0, 0)),
            spec_m,
            spec_m,
        ],
        out_shape=[
            jax.ShapeDtypeStruct((count, width_x, groups, width_y), F32),
            jax.ShapeDtypeStruct((count, 2, groups, width_y), BF16),
            jax.ShapeDtypeStruct((count, 2, groups, width_y), BF16),
        ],
        scratch_shapes=[pltpu.VMEM((groups * width_x, width_y), F32)],
        compiler_params=pltpu.CompilerParams(vmem_limit_bytes=24 << 20),
        cost_estimate=pl.CostEstimate(
            flops=40 * count * width_x * groups * width_y,
            bytes_accessed=8 * count * width_x * groups * width_y,
            transcendentals=0,
        ),
        name="transport_first",
    )(tracers, wind_x, wind_y, table)


def second_part(
    state, left, right, wind_x, wind_y, wind_l, wind_r, table, mean, start
):
    count, width_x, groups, width_y = state.shape
    step = 3
    skip = start // step
    spec_s = pl.BlockSpec((step, width_x, groups, width_y), lambda i: (i, 0, 0, 0))
    spec_m = pl.BlockSpec((step, 2, groups, width_y), lambda i: (i, 0, 0, 0))
    spec_w = pl.BlockSpec((step, width_x, width_y), lambda i: (i + skip, 0, 0))
    spec_n = pl.BlockSpec((step, 2, width_y), lambda i: (i + skip, 0, 0))
    return pl.pallas_call(
        lambda *refs: second_kernel(step, *refs),
        grid=(count // step,),
        in_specs=[
            spec_s, spec_m, spec_m, spec_w, spec_w, spec_n, spec_n,
            pl.BlockSpec(table.shape, lambda i: (0, 0)),
            pl.BlockSpec(mean.shape, lambda i: (0, 0)),
        ],
        out_specs=pl.BlockSpec(
            (step, len(TRIPLES), width_y, LANES), lambda i: (i, 0, 0, 0)
        ),
        out_shape=jax.ShapeDtypeStruct((count, len(TRIPLES), width_y, LANES), BF16),
        compiler_params=pltpu.CompilerParams(vmem_limit_bytes=24 << 20),
        cost_estimate=pl.CostEstimate(
            flops=40 * count * width_x * groups * width_y,
            bytes_accessed=8 * count * width_x * groups * width_y,
            transcendentals=0,
        ),
        name="transport_second",
    )(state, left, right, wind_x, wind_y, wind_l, wind_r, table, mean)


def align_kernel(n_fields, *refs):
    fields, out_ref, scratch = refs[:n_fields], refs[n_fields], refs[n_fields + 1]
    width_y = fields[0].shape[2]
    level = 0
    for field in fields:
        for l in range(field.shape[0]):
            scratch[pl.ds(level, width_y, stride=DEPTH), :] = field[l, 0].astype(F32)
            level += 1
    for l in range(level, DEPTH):
        scratch[pl.ds(l, width_y, stride=DEPTH), :] = jnp.zeros((width_y, LANES), F32)

    @pl.loop(0, width_y, unroll=8)
    def _(y):
        rows = pl.ds(pl.multiple_of(y * DEPTH, DEPTH), DEPTH)
        out_ref[0, rows, :] = scratch[rows, :].astype(BF16)


def align(fields):
    _, triples, width_y, lanes = fields[0].shape
    return pl.pallas_call(
        functools.partial(align_kernel, len(fields)),
        grid=(triples,),
        in_specs=[
            pl.BlockSpec((f.shape[0], 1, width_y, lanes), lambda g: (0, g, 0, 0)) for f in fields
        ],
        out_specs=pl.BlockSpec((1, width_y * DEPTH, lanes), lambda g: (g, 0, 0)),
        out_shape=jax.ShapeDtypeStruct((triples, width_y * DEPTH, lanes), BF16),
        scratch_shapes=[pltpu.VMEM((width_y * DEPTH, lanes), F32)],
        compiler_params=pltpu.CompilerParams(vmem_limit_bytes=24 << 20),
        cost_estimate=pl.CostEstimate(flops=1000, bytes_accessed=1000, transcendentals=0),
        name="align_columns",
    )(*fields)


def lanes_from(ref, k, rows, start):
    tile, shift = divmod(start, LANES)
    part = ref[k, rows, tile * LANES : (tile + 1) * LANES].astype(F32)
    if shift:
        part = pltpu.roll(part, LANES - shift, axis=1)
        if (tile + 2) * LANES <= ref.shape[2]:
            after = ref[k, rows, (tile + 1) * LANES : (tile + 2) * LANES].astype(F32)
            after = pltpu.roll(after, LANES - shift, axis=1)
            lane = lax.broadcasted_iota(jnp.int32, part.shape, 1)
            part = jnp.where(lane < LANES - shift, part, after)
    return part


def solve_kernel(
    pos_ref, value_hbm, block_hbm, out_ref,
    value_ref, block_ref, matrices, result, final, value_sem, block_sem,
):
    groups, rows, width_x, width_y = out_ref.shape
    levels = 2 * rows

    count, _, lanes = block_ref.shape

    def block_copy(k):
        return pltpu.make_async_copy(block_hbm.at[k], block_ref.at[k], block_sem.at[k])

    for k in range(count):
        block_copy(k).start()
    value_copy = pltpu.make_async_copy(value_hbm, value_ref, value_sem)
    value_copy.start()
    per_block = lanes // levels
    tall = -(-rows // 8) * 8

    @pl.loop(0, count, unroll=2)
    def _(k):
        block_copy(k).wait()
        for j in range(per_block):
            part = lanes_from(block_ref, k, slice(0, tall), j * levels)
            matrices[2 * k * per_block + j, :tall] = part.astype(BF16)
            part = lanes_from(block_ref, k, slice(2 * rows - tall, 2 * rows), j * levels)
            part = pltpu.roll(part, rows, axis=0)
            matrices[(2 * k + 1) * per_block + j, :tall] = part.astype(BF16)

    value_copy.wait()
    lane = lax.broadcasted_iota(jnp.int32, (rows, LANES), 1)
    eye = (
        lax.broadcasted_iota(jnp.int32, (LANES, LANES), 0)
        == lax.broadcasted_iota(jnp.int32, (LANES, LANES), 1)
    ).astype(F32).astype(BF16)
    for g, triple in enumerate(TRIPLES):

        @pl.loop(0, width_y, unroll=32)
        def _(y, g=g, triple=triple):
            columns = value_ref[g, pl.ds(pl.multiple_of(y * DEPTH, DEPTH), DEPTH), :]
            columns = jnp.concatenate(
                [columns, jnp.zeros((LANES - DEPTH, LANES), BF16)], axis=0
            )
            chosen = jnp.concatenate([matrices[pos_ref[x, y]] for x in triple], axis=0)
            product = jnp.dot(chosen, columns, preferred_element_type=F32)
            picked = product[(len(triple) - 1) * HEIGHT :][:rows]
            for i in range(len(triple) - 2, -1, -1):
                picked = jnp.where(
                    lane < (i + 1) * groups, product[i * HEIGHT : i * HEIGHT + rows], picked
                )
            result[pl.ds(y, rows, stride=width_y), :] = picked

        @pl.loop(0, rows, unroll=12)
        def _(a, triple=triple):
            start = pl.multiple_of(a * width_y, width_y)
            turned = lax.dot_general(
                eye,
                result[pl.ds(start, width_y), :].astype(BF16),
                (((1,), (1,)), ((), ())),
                preferred_element_type=F32,
            )
            for i, x in enumerate(triple):
                final[a, pl.ds(x, groups, stride=width_x), :] = turned[
                    i * groups : (i + 1) * groups
                ]

    @pl.loop(0, rows, unroll=4)
    def _(a):
        out_ref[:, a] = final[a].reshape(groups, width_x, width_y).astype(BF16)


def solve(value, block, position, shape):
    groups, rows, width_x, width_y = shape
    spans = 2 * block.shape[0] * (block.shape[2] // (2 * rows))
    anywhere = pl.BlockSpec(memory_space=pl.ANY)
    return pl.pallas_call(
        solve_kernel,
        in_specs=[pl.BlockSpec(memory_space=pltpu.SMEM), anywhere, anywhere],
        out_specs=pl.BlockSpec(memory_space=pltpu.VMEM),
        out_shape=jax.ShapeDtypeStruct(shape, BF16),
        scratch_shapes=[
            pltpu.VMEM(value.shape, BF16),
            pltpu.VMEM(block.shape, BF16),
            pltpu.VMEM((spans, HEIGHT, LANES), BF16),
            pltpu.VMEM((rows * width_y, LANES), F32),
            pltpu.VMEM((rows, groups * width_x, width_y), F32),
            pltpu.SemaphoreType.DMA(()),
            pltpu.SemaphoreType.DMA((block.shape[0],)),
        ],
        compiler_params=pltpu.CompilerParams(vmem_limit_bytes=58 << 20),
        cost_estimate=pl.CostEstimate(
            flops=4 * rows * rows * groups * width_x * width_y,
            bytes_accessed=12 << 20,
            transcendentals=0,
        ),
        name="solve_columns",
    )(position, value, block)


def elem_index(y, x, z):
    return (y % NY_CHIPS * NX_CHIPS + x % NX_CHIPS) * NZ_CHIPS + z % NZ_CHIPS


def fetch(value, dy=0, dx=0, dz=0):
    pairs = [
        (elem_index(y + dy, x + dx, z + dz), elem_index(y, x, z))
        for y in range(NY_CHIPS)
        for x in range(NX_CHIPS)
        for z in range(NZ_CHIPS)
    ]
    return lax.ppermute(value, ELEM, pairs)


def gather_matrices(block):
    near = [block] + [fetch(block, dz=d) for d in range(1, NZ_CHIPS)]
    half = NZ_CHIPS // 2
    halves = [jnp.concatenate(near[i : i + half], axis=1) for i in (0, half)]
    return lax.all_gather(jnp.concatenate(halves, axis=0), ("y", "x"), axis=0)


def span_position(span_ids, per_dev):
    owner, local = span_ids // per_dev, span_ids % per_dev
    dz = (owner % NZ_CHIPS - lax.axis_index("z")) % NZ_CHIPS
    return (owner // NZ_CHIPS * NZ_CHIPS + dz) * per_dev + local


def body(tracers, wind_x, wind_y, span_of, inverses):
    groups, half_levels, width_x, width_y = tracers.shape
    per_dev = inverses.shape[0]
    first_table, second_table, mean = table_y(width_y)
    size = NY_CHIPS * NX_CHIPS * NZ_CHIPS
    up = [(i, (i + 1) % size) for i in range(size)]
    down = [(j, i) for i, j in up]
    lev = lax.axis_index("lev")

    mine = lax.dynamic_slice_in_dim(inverses, lev * half_levels, half_levels, 1)
    own = lax.dynamic_slice_in_dim(mine, lev * half_levels, half_levels, 2)
    other = lax.dynamic_slice_in_dim(mine, (1 - lev) * half_levels, half_levels, 2)
    block = jnp.concatenate([own, other], axis=2).transpose(1, 0, 2)
    block = block.reshape(half_levels, -1)
    matrices = gather_matrices(block)
    position = span_position(span_of[:, 0], per_dev).reshape(width_x, width_y)

    wind_l = lax.ppermute(jnp.stack([wind_x[:, -1], wind_y[:, -1]], 1), ELEM, up)
    wind_r = lax.ppermute(jnp.stack([wind_x[:, 0], wind_y[:, 0]], 1), ELEM, down)

    count = half_levels // CHUNKS
    firsts = [
        first_part(tracers, wind_x, wind_y, first_table, i * count, count)
        for i in range(CHUNKS)
    ]
    own_fields, other_fields = [], []
    for i, (state, to_left, to_right) in enumerate(firsts):
        left = lax.ppermute(to_right, ELEM, up)
        right = lax.ppermute(to_left, ELEM, down)
        field = second_part(
            state, left, right, wind_x, wind_y, wind_l, wind_r, second_table, mean, i * count
        )
        own_fields.append(field)
        other_fields.append(lax.ppermute(field, "lev", [(0, 1), (1, 0)]))
    value = align(own_fields + other_fields)
    return solve(value, matrices, position, tracers.shape)


def solution(mesh):
    chips = jax.sharding.Mesh(
        mesh.devices.reshape(NY_CHIPS, NX_CHIPS, NZ_CHIPS, -1), ELEM + ("lev",)
    )
    return jax.shard_map(
        body,
        mesh=chips,
        in_specs=(
            P(None, "lev", ELEM, None),
            P("lev", ELEM, None),
            P("lev", ELEM, None),
            P(ELEM, None),
            P(ELEM, None, None),
        ),
        out_specs=P(None, "lev", ELEM, None),
        check_vma=False,
    )
```
